128 devices in a mesh: row: 8 (over x, z_hi), col: 4 (over y), rep: 4 (over z_lo, core).
Axes of the slice: x: 4, y: 4, z: 4 (z_hi: 2, z_lo: 2; z = z_hi * 2 + z_lo), core: 2. Of those that a mesh axis runs over, the one named last changes fastest.
Arguments:
- features: bfloat16 [65536, 256], P(('row', 'col', 'rep')), may hold values from -6 to 6
- blocks: bfloat16 [512, 128, 128, 128], P('row', ('col', 'rep')), may hold values from 0 to 0.015625
- block_cols: int32 [512, 128], P('row', ('col', 'rep')), may hold values from 0 to 31
- counts: int32 [512, 16], P('row', ('col', 'rep')), may hold values from 0 to 8, as said below
- weight: bfloat16 [256, 256], replicated, may hold values from -12 to 12
- bias: float32 [256], replicated, may hold values from -3 to 3
Outputs:
- hidden_out: bfloat16 [65536, 256], P(('row', 'col', 'rep'))
The draws below stay inside these ranges and needn't reach their ends.
Inputs may be any that keep to these rules, and one draw needn't show every extreme that they name: A block row's live slots in a column shard are its first counts slots.
All inputs are finite; a program needn't handle non-finite values.
Results may differ from the reference program's by a relative error of at most 0.02.
Values may be sent and summed in bfloat16 or wider, within the bound.
A program may use at most 192 MiB of HBM per device.

```python
import jax
import jax.numpy as jnp
from jax import lax

F = 256
BLK = 128
SLOTS = 8
ROWS_DEV = 512
NQ = 16
NODES = 65536
NBR = 512
BROWS = 64
CBLK = 32
N_ROW = 8
N_COL = 4
N_REP = 4


def draw_counts(key, part):
    key = jax.random.fold_in(key, 7)
    level_key, count_key = jax.random.split(key)
    levels = jax.random.randint(level_key, (N_ROW, 1, NQ), 1, SLOTS + 1)
    raw_counts = jax.random.randint(count_key, (N_ROW, BROWS, NQ), 0, SLOTS + 1)
    limited = jnp.minimum(raw_counts, levels).reshape(NBR, NQ)
    limited = limited.at[0, 0].set(SLOTS)
    return limited.astype(jnp.int32)


def touch_ends(drawn, rng, least, largest):
    dims = drawn.shape
    spot = [jax.random.randint(jax.random.fold_in(rng, axis), (), 0, dims[axis]) for axis in range(len(dims))]
    drawn = drawn.at[tuple(spot)].set(least)
    longest = dims.index(max(dims))
    spot[longest] = (spot[longest] + 1) % dims[longest]
    return drawn.at[tuple(spot)].set(largest)


def block_scale(rng, dims, cuts, low, largest):
    level = 1.0
    for dim, shards_of in cuts:
        heights = jax.random.uniform(jax.random.fold_in(jax.random.fold_in(rng, 6), dim), (shards_of,), jnp.float32, low / len(cuts), largest / len(cuts))
        level = level * jnp.repeat(jnp.exp(heights), dims[dim] // shards_of).reshape((-1,) + (1,) * (len(dims) - 1 - dim))
    return level


def gaussian(stream_key, dims, scale, reach, cuts=(), dtype=jnp.bfloat16):
    level = block_scale(stream_key, dims, cuts, -0.22, 0.18) if cuts else 1.0
    result = jax.random.normal(stream_key, dims, jnp.float32) * scale * level
    return jnp.minimum(jnp.maximum(result, -reach), reach).astype(dtype)


def setup_inputs(seed: int = 0) -> dict:
    splits = jax.random.split(jax.random.key(seed), 7)
    return {
        "features": gaussian(splits[0], (NODES, F), 1.0, 6.0, ((0, 128),)),
        "blocks": jnp.clip(0.015625 * jax.random.uniform(splits[1], (NBR, NQ * SLOTS, BLK, BLK), jnp.float32) ** block_scale(splits[1], (NBR, NQ * SLOTS, BLK, BLK), ((0, 8), (1, 16)), -0.2, 0.2), 0.0, 0.015625).astype(jnp.bfloat16),
        "block_cols": touch_ends(jax.random.randint(splits[2], (NBR, NQ * SLOTS), 0, CBLK), jax.random.fold_in(splits[2], 1), 0, CBLK - 1).astype(jnp.int32),
        "counts": draw_counts(jax.random.fold_in(splits[6], 71), 0),
        "weight": gaussian(splits[4], (F, F), 2.0, 12.0),
        "bias": gaussian(splits[5], (F,), 0.5, 3.0, (), jnp.float32),
    }


def reference(features, blocks, block_cols, counts, weight, bias):
    shard_total = N_COL * N_REP
    block_total = blocks.shape[0]
    row_sums = jnp.zeros((block_total, BLK), jnp.float32)
    for shard_number in range(shard_total):
        for slot_number in range(SLOTS):
            slot_live = counts[:, shard_number] > slot_number
            column = shard_number * SLOTS + slot_number
            block_sum = lax.optimization_barrier(jnp.sum(blocks[:, column].astype(jnp.float32), axis=2))
            row_sums = row_sums + jnp.where(slot_live[:, None], block_sum, jnp.float32(0.0))
    degree = 1.0 + row_sums.reshape(NODES)
    inverse_root = lax.rsqrt(degree)
    scaled = (inverse_root[:, None] * features.astype(jnp.float32)).astype(jnp.bfloat16)
    arranged = scaled.reshape(N_ROW, shard_total, ROWS_DEV, F)
    summed = jnp.zeros((block_total, BLK, F), jnp.float32)
    for shard_number in range(shard_total):
        shard_panel = arranged[:, shard_number].reshape(CBLK, BLK, F)
        shard_sum = jnp.zeros((block_total, BLK, F), jnp.float32)
        for slot_number in range(SLOTS):
            slot_live = counts[:, shard_number] > slot_number
            column = shard_number * SLOTS + slot_number
            picked = jnp.take(shard_panel, block_cols[:, column].astype(jnp.int32), axis=0)
            product = jnp.einsum('iab,ibf->iaf', blocks[:, column].astype(jnp.float32), picked.astype(jnp.float32))
            shard_sum = shard_sum + jnp.where(slot_live[:, None, None], product, jnp.float32(0.0))
        rounded = lax.optimization_barrier(shard_sum.astype(jnp.bfloat16))
        summed = summed + rounded.astype(jnp.float32)
    aggregated = (inverse_root[:, None] * (summed.reshape(NODES, F) + scaled.astype(jnp.float32))).astype(jnp.bfloat16)
    mixed = jnp.dot(aggregated, weight, preferred_element_type=jnp.float32) + bias.astype(jnp.float32)
    return jnp.maximum(mixed, 0.0).astype(jnp.bfloat16)
```

```python
import functools

import jax
import jax.numpy as jnp
from jax import lax
from jax.experimental import pallas as pl
from jax.experimental.pallas import tpu as pltpu
from jax.sharding import PartitionSpec as P

MESH = pl.DeviceIdType.MESH
BF16, F32 = jnp.bfloat16, jnp.float32
HALVES = 2
PRE = 6
MIDDLE = 12
GATHER_Z = 512
REDUCE_Z = 0
LAG = 2
ORDER = ((2, 0), (2, 1), (1, 0), (3, 0), (1, 1), (3, 1), (0, 0), (0, 1))


def kernel(cnt, cols, feat, blocks, weight, bias, out, blk, raw, pan, inv_t, rs_tx, rs_rx, inv_tx, inv_rx, part, sib_rx, acc,
           ab_rx, p_rx, m_rx, z_rx, agg, bsem, fsem, ssem, rsem):
    row, col, rep = lax.axis_index("row"), lax.axis_index("col"), lax.axis_index("rep")
    x, zh, zl, c = row // 2, row % 2, rep // 2, rep % 2
    q = col * 4 + rep
    n_chunk = 16
    brows = blk.shape[0] // n_chunk
    width = raw.shape[-1]

    def row_peer(i):
        return (lax.rem(row + i, 8), col, rep)

    def col_peer(i):
        p = lax.rem(q + i, 16)
        return (row, p // 4, p % 4)

    sib = (row, col, zl * 2 + 1 - c)
    y_next, y_prev = (row, lax.rem(col + 1, 4), rep), (row, lax.rem(col + 3, 4), rep)
    z_near = (row, col, (1 - zl) * 2 + c)
    x_next, x_prev = (lax.rem(x + 1, 4) * 2 + zh, col, rep), (lax.rem(x + 3, 4) * 2 + zh, col, rep)
    z_far = (x * 2 + 1 - zh, col, rep)

    barrier = pltpu.get_barrier_semaphore()
    for i in range(1, 8):
        pl.semaphore_signal(barrier, inc=1, device_id=row_peer(i), device_id_type=MESH)
    for i in range(1, 16):
        pl.semaphore_signal(barrier, inc=1, device_id=col_peer(i), device_id_type=MESH)

    feat_copies = []
    for h in range(HALVES):
        copy = pltpu.make_async_copy(feat.at[:, pl.ds(h * width, width)], raw.at[h, row], fsem.at[h])
        copy.start()
        feat_copies.append(copy)
    block_copies = []
    for k in range(n_chunk):
        here = pl.ds(k * brows, brows)
        copy = pltpu.make_async_copy(blocks.at[here], blk.at[here], bsem.at[k])
        copy.start()
        block_copies.append(copy)

    numbers, pending = {}, []

    def number(name):
        return numbers.setdefault(name, len(numbers))

    def send(name, src, dst, device):
        m = number(name)
        copy = pltpu.make_async_remote_copy(
            src_ref=src, dst_ref=dst, send_sem=ssem.at[m], recv_sem=rsem.at[m], device_id=device, device_id_type=MESH
        )
        copy.start()
        pending.append(copy)

    def recv(name, place):
        m = number(name)
        pltpu.make_async_remote_copy(
            src_ref=place, dst_ref=place, send_sem=ssem.at[m], recv_sem=rsem.at[m], device_id=sib, device_id_type=MESH
        ).wait_recv()

    rs_tx[...] = jnp.zeros_like(rs_tx)
    for h in range(HALVES):
        pan[h, 32] = jnp.zeros((128, width), BF16)

    def row_sums(k):
        block_copies[k].wait()
        for j in range(brows):
            i = k * brows + j
            live = cnt[0, i]
            total = jnp.zeros((128, 128), F32)
            for s in range(8):
                total = total + jnp.where(s < live, blk[i, s].astype(F32), 0.0)
            rs_tx[k, j : j + 1, :] = jnp.sum(total.T, axis=0, keepdims=True)

    ga, gb = 256 - GATHER_Z // 2, 256 + GATHER_Z // 2
    g_mid, g_outer = pl.ds(ga, GATHER_Z), (pl.ds(0, ga), pl.ds(gb, 512 - gb))
    at_next, at_prev, at_two = lax.rem(x + 1, 4), lax.rem(x + 3, 4), lax.rem(x + 2, 4)
    low, high = pl.ds(0, 256), pl.ds(256, 256)

    def piece(h, xs, z, rows):
        return raw.at[h, xs * 2 + z, rows]

    def outward(h, what, xs, sides=(0, 1)):
        if GATHER_Z < 512:
            for side in sides:
                here = piece(h, xs, zh, g_outer[side])
                send(("gzo", h, what, side), here, here, z_far)

    def gather_0(h):
        feat_copies[h].wait()
        own = raw.at[h, row]
        mid = piece(h, x, zh, g_mid)
        send(("gx+", h), own, own, x_next)
        send(("gx-", h), own, own, x_prev)
        send(("gz", h), mid, mid, z_far)
        outward(h, 0, x)

    def gather_1(h):
        mid = piece(h, x, 1 - zh, g_mid)
        recv(("gz", h), mid)
        send(("gzx+", h), mid, mid, x_next)
        send(("gzx-", h), mid, mid, x_prev)
        recv(("gx+", h), raw.at[h, at_prev * 2 + zh])
        here = piece(h, at_prev, zh, low)
        send(("gxx+", h), here, here, x_next)
        recv(("gx-", h), raw.at[h, at_next * 2 + zh])
        here = piece(h, at_next, zh, high)
        send(("gxx-", h), here, here, x_prev)
        outward(h, 1, at_prev)
        outward(h, 2, at_next)

    def gather_2(h):
        recv(("gzx+", h), piece(h, at_prev, 1 - zh, g_mid))
        here = piece(h, at_prev, 1 - zh, pl.ds(ga, 256 - ga))
        send(("gzxx+", h), here, here, x_next)
        recv(("gzx-", h), piece(h, at_next, 1 - zh, g_mid))
        here = piece(h, at_next, 1 - zh, pl.ds(256, gb - 256))
        send(("gzxx-", h), here, here, x_prev)
        recv(("gxx+", h), piece(h, at_two, zh, low))
        outward(h, 3, at_two, (0,))
        recv(("gxx-", h), piece(h, at_two, zh, high))
        outward(h, 3, at_two, (1,))

    def gather_3(h):
        recv(("gzxx+", h), piece(h, at_two, 1 - zh, pl.ds(ga, 256 - ga)))
        recv(("gzxx-", h), piece(h, at_two, 1 - zh, pl.ds(256, gb - 256)))
        if GATHER_Z < 512:
            for what, xs in enumerate((x, at_prev, at_next, at_two)):
                for side in (0, 1):
                    recv(("gzo", h, what, side), piece(h, xs, 1 - zh, g_outer[side]))

    def scale(h):
        def group(r, _):
            for j in range(4):
                rows = pl.ds(j * 128, 128)
                factor = inv_t[r, :, j : j + 1]
                pan[h, r * 4 + j] = (raw[h, r, rows, :].astype(F32) * factor).astype(BF16)
            return 0

        lax.fori_loop(0, 8, group, 0, unroll=2)

    def product(h, slot, side, chip, core):
        first = (chip * 2 + core) * 4
        for j in range(4):
            i = first + j
            live = cnt[0, i]
            picked = jnp.concatenate([pan[h, jnp.where(s < live, cols[s, i], 32)] for s in range(8)], axis=0)
            tile = jnp.concatenate([blk[i, s] for s in range(8)], axis=1)
            part[h, slot, side, pl.ds(j * 128, 128), :] = jnp.dot(tile, picked, preferred_element_type=F32).astype(BF16)

    def unit(h, off, zc):
        slot = off * 2 + zc
        chip = lax.rem(col + off, 4) * 2 + (zl if zc else 1 - zl)
        product(h, slot, 0, chip, 1 - c)
        send(("sib", h, slot), part.at[h, slot, 0], sib_rx.at[h, slot], sib)
        product(h, slot, 1, chip, c)

    ra, rb = 256 - REDUCE_Z // 2, 256 + REDUCE_Z // 2
    ranges = [(lo, hi) for lo, hi in ((0, ra), (ra, 256), (256, rb), (rb, 512)) if hi > lo]

    def moved(name, h, off, zc, src, dst, device, lo, hi):
        if hi > lo:
            rows = pl.ds(lo, hi - lo)
            send((name, h, off, zc, lo), src.at[rows], dst.at[rows], device)

    def arrived(name, h, off, zc, dst, lo, hi):
        if hi > lo:
            recv((name, h, off, zc, lo), dst.at[pl.ds(lo, hi - lo)])

    def combine(h, off, zc):
        slot = off * 2 + zc
        last = zc == 1 and off == 0
        recv(("sib", h, slot), sib_rx.at[h, slot])
        cuts = ((0, 512),) if zc else ((0, ra), (rb, 512))
        if off == 1:
            arrived("ab+", h, 2, zc, ab_rx.at[h, zc], 0, 256 if zc else ra)
        if off == 3:
            arrived("ab-", h, 2, zc, ab_rx.at[h, zc], 256 if zc else rb, 512)
        if off == 0:
            for lo, hi in cuts:
                arrived("p", h, 1, zc, p_rx.at[h, zc], lo, hi)
                arrived("m", h, 3, zc, m_rx.at[h, zc], lo, hi)
        if zc == 1:
            arrived("zm", h, off, 0, z_rx.at[h, off], ra, rb)
            if off == 0:
                arrived("zo", h, off, 0, z_rx.at[h, off], 0, ra)
                arrived("zo", h, off, 0, z_rx.at[h, off], rb, 512)
        sums = []
        for lo, hi in ranges:
            rows = pl.ds(lo, hi - lo)
            mid = lo >= ra and hi <= rb
            total = part[h, slot, 1, rows, :].astype(F32) + sib_rx[h, slot, rows, :].astype(F32)
            if (off == 1 and hi <= 256 or off == 3 and lo >= 256) and (zc == 1 or not mid):
                total = total + ab_rx[h, zc, rows, :].astype(F32)
            if off == 0 and (zc == 1 or not mid):
                total = total + p_rx[h, zc, rows, :].astype(F32) + m_rx[h, zc, rows, :].astype(F32)
            if zc == 1 and (mid or off == 0):
                total = total + z_rx[h, off, rows, :].astype(F32)
            if last:
                sums.append(total)
            else:
                acc[h, slot, rows, :] = total.astype(BF16)
        if last:
            return jnp.concatenate(sums, axis=0)
        src = acc.at[h, slot]
        if zc == 0:
            moved("zm", h, off, zc, src, z_rx.at[h, off], z_near, ra, rb)
        if off == 2:
            moved("ab+", h, off, zc, src, ab_rx.at[h, zc], y_next, 0, 256 if zc else ra)
            moved("ab-", h, off, zc, src, ab_rx.at[h, zc], y_prev, 256 if zc else rb, 512)
        for lo, hi in cuts:
            if off == 1:
                moved("p", h, off, zc, src, p_rx.at[h, zc], y_next, lo, hi)
            if off == 3:
                moved("m", h, off, zc, src, m_rx.at[h, zc], y_prev, lo, hi)
            if off == 0:
                moved("zo", h, off, zc, src, z_rx.at[h, off], z_near, lo, hi)
        return None

    def finish(h, total):
        for j in range(4):
            rows = slice(j * 128, j * 128 + 128)
            factor = inv_t[8, :, j : j + 1]
            own = pan[h, row * 4 + j].astype(F32)
            agg[rows, h * width : (h + 1) * width] = (factor * (total[rows] + own)).astype(BF16)

    for k in range(PRE):
        row_sums(k)
    pl.semaphore_wait(barrier, 22)
    gather_0(0)
    for k in range(PRE, MIDDLE):
        row_sums(k)
    gather_1(0)
    gather_0(1)
    for k in range(MIDDLE, n_chunk):
        row_sums(k)
    for i in range(1, 16):
        to = lax.rem(q + i, 16)
        send(("rs", i), rs_tx.at[to], rs_rx.at[q], col_peer(i))
    rs_rx[q] = rs_tx[q]
    gather_2(0)
    for i in range(1, 16):
        recv(("rs", i), rs_rx.at[lax.rem(q + 16 - i, 16)])
    degree = rs_rx[0]
    for i in range(1, 16):
        degree = degree + rs_rx[i]
    inv_tx[...] = lax.rsqrt(1.0 + degree)
    for i in range(1, 8):
        send(("inv", i), inv_tx, inv_rx.at[row], row_peer(i))
    inv_rx[row] = inv_tx[...]
    gather_1(1)
    for i in range(1, 8):
        recv(("inv", i), inv_rx.at[lax.rem(row + 8 - i, 8)])
    for r in range(8):
        inv_t[r] = inv_rx[r].T
    inv_t[8] = inv_tx[...].T
    gather_3(0)
    scale(0)

    waiting = []
    for h in range(HALVES):
        if h == 1:
            gather_3(1)
            scale(1)
        for n, (off, zc) in enumerate(ORDER):
            unit(h, off, zc)
            waiting.append((h, off, zc))
            if h == 0 and n == 1:
                gather_2(1)
            if len(waiting) > LAG:
                h_, off_, zc_ = waiting.pop(0)
                total = combine(h_, off_, zc_)
                if total is not None:
                    finish(h_, total)
    for h_, off_, zc_ in waiting:
        total = combine(h_, off_, zc_)
        if total is not None:
            finish(h_, total)
    mixed = jnp.dot(agg[...], weight[...], preferred_element_type=F32) + bias[...]
    out[...] = jnp.maximum(mixed, 0.0).astype(BF16)
    for copy in pending:
        copy.wait_send()
    assert len(numbers) <= ssem.shape[0]


def shards(features, blocks, block_cols, counts, weight, bias):
    rows, width = features.shape
    half = width // HALVES
    vmem, smem, anywhere = (pl.BlockSpec(memory_space=s) for s in (pltpu.VMEM, pltpu.SMEM, pl.ANY))
    dma = pltpu.SemaphoreType.DMA
    return pl.pallas_call(
        kernel,
        out_shape=jax.ShapeDtypeStruct((rows, width), BF16),
        in_specs=[smem, smem, anywhere, anywhere, vmem, vmem],
        out_specs=vmem,
        scratch_shapes=[
            pltpu.VMEM(blocks.shape, BF16),
            pltpu.VMEM((HALVES, 8, rows, half), BF16),
            pltpu.VMEM((HALVES, 33, 128, half), BF16),
            pltpu.VMEM((9, 128, 8), F32),
            pltpu.VMEM((16, 8, 128), F32),
            pltpu.VMEM((16, 8, 128), F32),
            pltpu.VMEM((8, 128), F32),
            pltpu.VMEM((8, 8, 128), F32),
            pltpu.VMEM((HALVES, 8, 2, rows, half), BF16),
            pltpu.VMEM((HALVES, 8, rows, half), BF16),
            pltpu.VMEM((HALVES, 8, rows, half), BF16),
            pltpu.VMEM((HALVES, 2, rows, half), BF16),
            pltpu.VMEM((HALVES, 2, rows, half), BF16),
            pltpu.VMEM((HALVES, 2, rows, half), BF16),
            pltpu.VMEM((HALVES, 4, rows, half), BF16),
            pltpu.VMEM((rows, width), BF16),
            dma((16,)), dma((HALVES,)), dma((128,)), dma((128,)),
        ],
        compiler_params=pltpu.CompilerParams(collective_id=0, has_side_effects=True, vmem_limit_bytes=58 << 20),
        cost_estimate=pl.CostEstimate(flops=4_300_000_000, bytes_accessed=17_000_000, transcendentals=1024),
    )(counts.T, block_cols.T, features, blocks, weight, bias.reshape(1, width))


def solution(mesh):
    return jax.shard_map(
        shards,
        mesh=mesh,
        in_specs=(
            P(("row", "col", "rep"), None),
            P("row", ("col", "rep"), None, None),
            P("row", ("col", "rep")),
            P("row", ("col", "rep")),
            P(),
            P(),
        ),
        out_specs=P(("row", "col", "rep"), None),
        check_vma=False,
    )
```

```python
import contextlib
import math

import jax
import jax.numpy as jnp
from jax import lax
from jax.experimental import pallas as pl
from jax.experimental.pallas import tpu as pltpu
from jax.sharding import PartitionSpec as P

MESH = pl.DeviceIdType.MESH
BF16, F32 = jnp.bfloat16, jnp.float32
HALVES = 2
SCOPES = False
PRE = 3
GATHER_Z = 384
REDUCE_Z = (0, 0)
DEPTH = 6
FILL = 9
EARLY = 0
CHUNKS = ((2, 1, 0), (2, 1, 1), (2, 0, 0), (2, 0, 1), (1, 1, 0), (1, 1, 1), (3, 1, 0), (3, 1, 1), (1, 0, 0), (1, 0, 1), (3, 0, 0),
          (3, 0, 1), (0, 1, 0), (0, 1, 1), (0, 0, 1), (0, 0, 0))
N_SEM = 66 + 16 * (GATHER_Z < 512) + 8 * (REDUCE_Z[1] > 0)
UNITS = (((2, 0), (2, 1)), ((1, 0), (3, 0)), ((1, 1), (3, 1)), ((0, 0), (0, 1)))
FAR = ((2, 0, 0), (2, 0, 1), (2, 1, 0), (2, 1, 1))
NEAR = [((1, zc, 1), (3, zc, 0)) for zc in (0, 1)]
NEXT = [((1, zc, 0), (3, zc, 1)) for zc in (0, 1)]
HOME = [((0, zc, 0), (0, zc, 1)) for zc in (0, 1)]


def schedule():
    def close(h, *groups):
        return [("close", h, *which) for group in groups for which in group]

    steps = [("sums", k) for k in range(PRE)] + [("barrier",), ("g_own", 0, 0), ("g_far", 0), ("g_own", 0, 1)]
    steps += [("sums", k) for k in range(PRE, FILL)] + [("g_own", 1, 0)]
    steps += [("sums", k) for k in range(FILL, 16)]
    steps += [("g_relay", 0), ("g_z", 0), ("send_roots",), ("g_far", 1)] + [("g_relay", 1), ("g_own", 1, 1)] * EARLY
    steps += [("g_out", 0), ("g_zrelay", 0)] + [("g_relay", 1), ("g_own", 1, 1)] * (not EARLY)
    steps += [("inputs",), ("turn_roots",), ("scale", 0, 0), ("g_z", 1), ("g_rest", 0), ("scale", 0, 1)]
    steps += [("unit", 0, 0), ("g_out", 1), ("unit", 0, 1), *close(0, FAR), ("g_zrelay", 1), ("unit", 0, 2), *close(0, NEAR[0])]
    steps += [("unit", 0, 3), ("scale", 1, 0), *close(0, NEXT[0], NEAR[1], NEXT[1]), ("g_rest", 1), ("scale", 1, 1)]
    steps += [("unit", 1, 0), ("unit", 1, 1), *close(1, FAR[:2]), *close(0, HOME[0]), ("unit", 1, 2), *close(1, NEAR[0])]
    steps += [*close(1, FAR[2:]), ("unit", 1, 3), *close(1, NEXT[0], NEAR[1]), *close(0, HOME[1]), *close(1, NEXT[1], HOME[0])]
    steps += [("drain",), *close(1, HOME[1][:1]), ("output", 0), *close(1, HOME[1][1:]), ("output", 1), ("leave",)]
    return steps


def kernel(cnt_in, cols_in, feat, blocks, weight_in, bias_in, out, cnt, cols, weight, bias, o_v, blk, raw, pan, inv_t, rs_tx, rs_rx, inv_tx, inv_rx, part, sib_rx, acc,
           ab_rx, p_rx, m_rx, z_rx, agg, isem, osem, bsem, fsem, ssem, rsem):
    row, col, rep = lax.axis_index("row"), lax.axis_index("col"), lax.axis_index("rep")
    x, zh, zl, c = row // 2, row % 2, rep // 2, rep % 2
    q = col * 4 + rep
    n_chunk = 16
    brows = blk.shape[0] // n_chunk
    width = raw.shape[-1]

    def row_peer(i):
        return (lax.rem(row + i, 8), col, rep)

    def col_peer(i):
        p = lax.rem(q + i, 16)
        return (row, p // 4, p % 4)

    sib = (row, col, zl * 2 + 1 - c)
    y_next, y_prev = (row, lax.rem(col + 1, 4), rep), (row, lax.rem(col + 3, 4), rep)
    z_near = (row, col, (1 - zl) * 2 + c)
    x_next, x_prev = (lax.rem(x + 1, 4) * 2 + zh, col, rep), (lax.rem(x + 3, 4) * 2 + zh, col, rep)
    z_far = (x * 2 + 1 - zh, col, rep)

    def start(src, dst, sem):
        copy = pltpu.make_async_copy(src, dst, sem)
        copy.start()
        return copy

    feat_copies = [start(feat.at[:, pl.ds(h * width, width)], raw.at[h, row], fsem.at[h]) for h in range(HALVES)]
    cnt_copy = start(cnt_in, cnt, isem.at[0])

    block_copies = []

    def place_of(dy, dz, dc):
        return lax.rem(col + dy, 4), zl + dz - 2 * dz * zl, c + dc - 2 * dc * c

    def chunk_rows(k):
        y_, z_, c_ = place_of(*CHUNKS[k])
        return (y_ * 4 + z_ * 2 + c_) * brows

    def fetch(k):
        here = pl.ds(chunk_rows(k), brows)
        block_copies.append(start(blocks.at[here], blk.at[here], bsem.at[k % DEPTH]))

    barrier = pltpu.get_barrier_semaphore()
    fetch(0)
    for i in range(1, 8):
        pl.semaphore_signal(barrier, inc=1, device_id=row_peer(i), device_id_type=MESH)
    fetch(1)
    for i in range(1, 16):
        pl.semaphore_signal(barrier, inc=1, device_id=col_peer(i), device_id_type=MESH)
    for k in range(2, DEPTH):
        fetch(k)
    late_copies = [
        start(src, dst, isem.at[i + 1]) for i, (src, dst) in enumerate(((cols_in, cols), (weight_in, weight), (bias_in, bias)))
    ]

    numbers, pending = {}, [0, 0]

    def number(name):
        return numbers.setdefault(name, len(numbers))

    def send(name, src, dst, device, small=0):
        pltpu.make_async_remote_copy(
            src_ref=src, dst_ref=dst, send_sem=ssem.at[small], recv_sem=rsem.at[number(name)], device_id=device, device_id_type=MESH
        ).start()
        pending[small] += math.prod(src.shape) * src.dtype.itemsize

    def recv(name, place):
        pltpu.make_async_copy(place, place, rsem.at[number(name)]).wait()

    rs_tx[...] = jnp.zeros_like(rs_tx)
    for h in range(HALVES):
        pan[h, 32] = jnp.zeros((128, width), BF16)

    def row_sums(k):
        if k == 0:
            cnt_copy.wait()
        block_copies[k].wait()
        if k + DEPTH < n_chunk:
            fetch(k + DEPTH)
        first = chunk_rows(k)
        for j in range(brows):
            i = first + j
            live = cnt[0, i]
            total = jnp.zeros((128, 128), F32)
            for s in range(8):
                total = total + jnp.where(s < live, blk[i, s].astype(F32), 0.0)
            rs_tx[k, j : j + 1, :] = jnp.sum(total.T, axis=0, keepdims=True)
        if k >= PRE:
            send_sum(k)

    def send_sum(k):
        if k < n_chunk - 1:
            y_, z_, c_ = place_of(*CHUNKS[k])
            send("sums", rs_tx.at[k], rs_rx.at[q], (row, y_, z_ * 2 + c_), small=1)
        else:
            rs_rx[q] = rs_tx[k]

    half_z = GATHER_Z // 2
    mid = (pl.ds(256 - half_z, half_z), pl.ds(256, half_z))
    outer = (pl.ds(0, 256 - half_z), pl.ds(256 + half_z, 256 - half_z))
    side_rows = (pl.ds(0, 256), pl.ds(256, 256))
    at_next, at_prev, at_two = lax.rem(x + 1, 4), lax.rem(x + 3, 4), lax.rem(x + 2, 4)

    def piece(h, xs, z, rows):
        return raw.at[h, xs * 2 + z, rows]

    def copied(name, h, place, device):
        send((name, h), place, place, device)

    def outward(h, what, xs, side):
        if GATHER_Z < 512:
            copied(("out", what, side), h, piece(h, xs, zh, outer[side]), z_far)

    def gather_own(h, part):
        if part == 0:
            feat_copies[h].wait()
        copied(("own+", part), h, piece(h, x, zh, side_rows[part]), x_next)
        copied(("own-", 1 - part), h, piece(h, x, zh, side_rows[1 - part]), x_prev)

    def gather_far(h):
        for side in (0, 1):
            copied(("z", side), h, piece(h, x, zh, mid[side]), z_far)
        for side in (0, 1):
            outward(h, 0, x, side)

    def gather_relay(h):
        recv((("own+", 0), h), piece(h, at_prev, zh, side_rows[0]))
        copied("relay+", h, piece(h, at_prev, zh, side_rows[0]), x_next)
        recv((("own-", 1), h), piece(h, at_next, zh, side_rows[1]))
        copied("relay-", h, piece(h, at_next, zh, side_rows[1]), x_prev)
        outward(h, 1, at_prev, 0)
        outward(h, 2, at_next, 1)

    def gather_z(h):
        for side in (0, 1):
            place = piece(h, x, 1 - zh, mid[side])
            recv((("z", side), h), place)
            copied(("z+", side), h, place, x_next)
            copied(("z-", side), h, place, x_prev)

    def gather_out(h):
        recv((("own+", 1), h), piece(h, at_prev, zh, side_rows[1]))
        outward(h, 1, at_prev, 1)
        recv((("own-", 0), h), piece(h, at_next, zh, side_rows[0]))
        outward(h, 2, at_next, 0)

    def gather_zrelay(h):
        place = piece(h, at_prev, 1 - zh, mid[0])
        recv((("z+", 0), h), place)
        copied("zrelay+", h, place, x_next)
        place = piece(h, at_next, 1 - zh, mid[1])
        recv((("z-", 1), h), place)
        copied("zrelay-", h, place, x_prev)
        recv(("relay+", h), piece(h, at_two, zh, side_rows[0]))
        outward(h, 3, at_two, 0)
        recv(("relay-", h), piece(h, at_two, zh, side_rows[1]))
        outward(h, 3, at_two, 1)

    def gather_rest(h):
        recv((("z+", 1), h), piece(h, at_prev, 1 - zh, mid[1]))
        recv((("z-", 0), h), piece(h, at_next, 1 - zh, mid[0]))
        recv(("zrelay+", h), piece(h, at_two, 1 - zh, mid[0]))
        recv(("zrelay-", h), piece(h, at_two, 1 - zh, mid[1]))
        if GATHER_Z < 512:
            for what, xs in enumerate((x, at_prev, at_next, at_two)):
                for side in (0, 1):
                    recv((("out", what, side), h), piece(h, xs, 1 - zh, outer[side]))

    def scale(h, part):
        def group(xs, z):
            r = xs * 2 + z
            for j in range(4):
                rows = pl.ds(j * 128, 128)
                factor = inv_t[r, :, j : j + 1]
                pan[h, r * 4 + j] = (raw[h, r, rows, :].astype(F32) * factor).astype(BF16)

        if part == 0:
            for xs in (x, at_prev, at_next, at_two):
                group(xs, zh)
        else:
            for xs in (x, at_prev, at_next, at_two):
                group(xs, 1 - zh)

    def product(halves, slot, side, chip, core):
        first = (chip * 2 + core) * 4
        for j in range(4):
            i = first + j
            live = cnt[0, i]
            at = [jnp.where(s < live, cols[s, i], 32) for s in range(8)]
            picked = jnp.concatenate(
                [jnp.concatenate([pan[h, at[s]] for s in range(8)], axis=0) for h in halves], axis=1
            )
            tile = jnp.concatenate([blk[i, s] for s in range(8)], axis=1)
            total = jnp.dot(tile, picked, preferred_element_type=F32).astype(BF16)
            for n, h in enumerate(halves):
                part[h, side, slot, pl.ds(j * 128, 128), :] = total[:, n * width : (n + 1) * width]

    def unit(h, number):
        pairs = UNITS[number]
        for side, core in ((0, 1 - c), (1, c)):
            for n, (off, zc) in enumerate(pairs):
                chip = lax.rem(col + off, 4) * 2 + (zl if zc else 1 - zl)
                product((h,), number * 2 + n, side, chip, core)
        here = pl.ds(number * 2, 2)
        send(("sib", h, number), part.at[h, 0, here], sib_rx.at[h, here], sib)

    at_home = set()

    def moved(name, src, dst, device, lo, hi):
        if hi > lo:
            rows = pl.ds(lo, hi - lo)
            send(name, src.at[rows], dst.at[rows], device)

    def arrived(name, dst, lo, hi):
        if hi > lo:
            recv(name, dst.at[pl.ds(lo, hi - lo)])

    def close(h, off, zc, side):
        number, n = next((u, p.index((off, zc))) for u, p in enumerate(UNITS) if (off, zc) in p)
        slot = number * 2 + n
        last = zc == 1 and off == 0
        if (h, number) not in at_home:
            at_home.add((h, number))
            recv(("sib", h, number), sib_rx.at[h, pl.ds(number * 2, 2)])
        ra, rb = 256 - REDUCE_Z[h] // 2, 256 + REDUCE_Z[h] // 2
        outer_r, mid_r = ((0, ra), (ra, 256)) if side == 0 else ((rb, 512), (256, rb))
        lo, hi = (side * 256, side * 256 + 256) if zc else outer_r
        takes_ab = (off, side) in ((1, 0), (3, 1))
        if takes_ab:
            arrived(("ab", h, zc, side), ab_rx.at[h, zc], lo, hi)
        if off == 0:
            arrived(("p", h, zc, side), p_rx.at[h, zc], lo, hi)
            arrived(("m", h, zc, side), m_rx.at[h, zc], lo, hi)
        if zc == 1:
            arrived(("zm", h, off, side), z_rx.at[h, off], *mid_r)
            if off == 0:
                arrived(("zo", h, off, side), z_rx.at[h, off], *outer_r)
        for is_mid, (a, b) in enumerate((outer_r, mid_r)):
            if b == a:
                continue
            rows = pl.ds(a, b - a)
            round_y = zc == 1 or not is_mid
            total = part[h, 1, slot, rows, :].astype(F32) + sib_rx[h, slot, rows, :].astype(F32)
            if takes_ab and round_y:
                total = total + ab_rx[h, zc, rows, :].astype(F32)
            if off == 0 and round_y:
                total = total + p_rx[h, zc, rows, :].astype(F32) + m_rx[h, zc, rows, :].astype(F32)
            if zc == 1 and (is_mid or off == 0):
                total = total + z_rx[h, off, rows, :].astype(F32)
            if last:
                finish(h, a, b, total)
            else:
                acc[h, slot, rows, :] = total.astype(BF16)
        src = acc.at[h, slot]
        if zc == 0:
            moved(("zm", h, off, side), src, z_rx.at[h, off], z_near, *mid_r)
            if off == 0:
                moved(("zo", h, off, side), src, z_rx.at[h, off], z_near, *outer_r)
        if off == 2:
            moved(("ab", h, zc, side), src, ab_rx.at[h, zc], y_prev if side else y_next, lo, hi)
        if off == 1:
            moved(("p", h, zc, side), src, p_rx.at[h, zc], y_next, lo, hi)
        if off == 3:
            moved(("m", h, zc, side), src, m_rx.at[h, zc], y_prev, lo, hi)

    def finish(h, a, b, total):
        while a < b:
            j, end = a // 128, min(b, a // 128 * 128 + 128)
            factor = inv_t[8, a - j * 128 : end - j * 128, j : j + 1]
            own = pan[h, row * 4 + j, a - j * 128 : end - j * 128, :].astype(F32)
            agg[a:end, h * width : (h + 1) * width] = (factor * (total[: end - a] + own)).astype(BF16)
            total, a = total[end - a :], end

    def output(side):
        for j in (side * 2, side * 2 + 1):
            rows = pl.ds(j * 128, 128)
            mixed = jnp.dot(agg[rows, :], weight[...], preferred_element_type=F32) + bias[...]
            o_v[rows, :] = jnp.maximum(mixed, 0.0).astype(BF16)
            out_copies.append(start(o_v.at[rows], out.at[rows], osem.at[j]))

    out_copies = []

    def leave():
        for copy in out_copies:
            copy.wait()

    def drain():
        for n, (ref, unit_bytes) in enumerate(((blk, blk.shape[1] * 128 * 256), (o_v, o_v.shape[1] * 2))):
            assert pending[n] % unit_bytes == 0
            here = ref.at[pl.ds(0, pending[n] // unit_bytes)]
            pltpu.make_async_copy(here, here, ssem.at[n]).wait()

    def inputs():
        for copy in late_copies:
            copy.wait()

    def send_roots():
        recv("sums", rs_rx.at[pl.ds(0, 15)])
        degree = rs_rx[0]
        for i in range(1, 16):
            degree = degree + rs_rx[i]
        inv_tx[...] = lax.rsqrt(1.0 + degree)
        for i in range(1, 8):
            send("roots", inv_tx, inv_rx.at[row], row_peer(i), small=1)
        inv_rx[row] = inv_tx[...]

    def turn_roots():
        recv("roots", inv_rx.at[pl.ds(0, 7)])
        for r in range(8):
            inv_t[r] = inv_rx[r].T
        inv_t[8] = inv_tx[...].T

    def pass_barrier():
        pl.semaphore_wait(barrier, 22)
        for k in range(PRE):
            send_sum(k)

    work = {
        "sums": row_sums, "barrier": pass_barrier, "g_own": gather_own, "g_relay": gather_relay, "g_far": gather_far, "g_z": gather_z, "g_out": gather_out,
        "g_zrelay": gather_zrelay, "g_rest": gather_rest, "send_roots": send_roots,
        "turn_roots": turn_roots, "scale": scale, "unit": unit, "close": close, "output": output, "leave": leave,
        "drain": drain, "inputs": inputs,
    }
    for name, *args in schedule():
        with jax.named_scope("_".join(map(str, (name, *args)))) if SCOPES else contextlib.nullcontext():
            work[name](*args)
    assert len(numbers) == N_SEM, len(numbers)


def shards(features, blocks, block_cols, counts, weight, bias):
    rows, width = features.shape
    half = width // HALVES
    anywhere = pl.BlockSpec(memory_space=pl.ANY)
    dma = pltpu.SemaphoreType.DMA
    return pl.pallas_call(
        kernel,
        out_shape=jax.ShapeDtypeStruct((rows, width), BF16),
        in_specs=[anywhere] * 6,
        out_specs=anywhere,
        scratch_shapes=[
            pltpu.SMEM((1, blocks.shape[0]), jnp.int32),
            pltpu.SMEM((8, blocks.shape[0]), jnp.int32),
            pltpu.VMEM((width, width), BF16),
            pltpu.VMEM((1, width), F32),
            pltpu.VMEM((rows, width), BF16),
            pltpu.VMEM(blocks.shape, BF16),
            pltpu.VMEM((HALVES, 8, rows, half), BF16),
            pltpu.VMEM((HALVES, 33, 128, half), BF16),
            pltpu.VMEM((9, 128, 8), F32),
            pltpu.VMEM((16, 8, 128), F32),
            pltpu.VMEM((16, 8, 128), F32),
            pltpu.VMEM((8, 128), F32),
            pltpu.VMEM((8, 8, 128), F32),
            pltpu.VMEM((HALVES, 2, 8, rows, half), BF16),
            pltpu.VMEM((HALVES, 8, rows, half), BF16),
            pltpu.VMEM((HALVES, 8, rows, half), BF16),
            pltpu.VMEM((HALVES, 2, rows, half), BF16),
            pltpu.VMEM((HALVES, 2, rows, half), BF16),
            pltpu.VMEM((HALVES, 2, rows, half), BF16),
            pltpu.VMEM((HALVES, 4, rows, half), BF16),
            pltpu.VMEM((rows, width), BF16),
            dma((4,)), dma((4,)), dma((DEPTH,)), dma((HALVES,)), dma((2,)), dma((N_SEM,)),
        ],
        compiler_params=pltpu.CompilerParams(collective_id=0, has_side_effects=True, vmem_limit_bytes=58 << 20),
        cost_estimate=pl.CostEstimate(flops=4_300_000_000, bytes_accessed=17_000_000, transcendentals=1024),
    )(counts.T, block_cols.T, features, blocks, weight, bias.reshape(1, width))


def solution(mesh):
    return jax.shard_map(
        shards,
        mesh=mesh,
        in_specs=(
            P(("row", "col", "rep"), None),
            P("row", ("col", "rep"), None, None),
            P("row", ("col", "rep")),
            P("row", ("col", "rep")),
            P(),
            P(),
        ),
        out_specs=P(("row", "col", "rep"), None),
        check_vma=False,
    )
```

```python
import contextlib
import math

import jax
import jax.numpy as jnp
from jax import lax
from jax.experimental import pallas as pl
from jax.experimental.pallas import tpu as pltpu
from jax.sharding import PartitionSpec as P

MESH = pl.DeviceIdType.MESH
BF16, F32 = jnp.bfloat16, jnp.float32
HALVES = 2
SCOPES = False
PRE = 3
GATHER_Z = 384
STALL = 0
FAR_SOON = 1
REDUCE_Z = (0, 128)
DEPTH = 6
FILL = 9
CHUNKS = tuple((dy, dz, dc) for dz in (1, 0) for dy in (2, 1, 3, 0) for dc in (0, 1))
CHUNKS = CHUNKS[:-2] + CHUNKS[:-3:-1]
N_SEM = 66 + 16 * (GATHER_Z < 512) + 8 * sum(z > 0 for z in REDUCE_Z)
UNITS = (((2, 0), (2, 1)), ((1, 0), (3, 0)), ((1, 1), (3, 1)), ((0, 0), (0, 1)))
FAR = ((2, 0, 0), (2, 0, 1), (2, 1, 0), (2, 1, 1))
NEAR = [((1, zc, 1), (3, zc, 0)) for zc in (0, 1)]
NEXT = [((1, zc, 0), (3, zc, 1)) for zc in (0, 1)]
HOME = [((0, zc, 0), (0, zc, 1)) for zc in (0, 1)]


def schedule():
    def close(h, *groups):
        return [("close", h, *which) for group in groups for which in group]

    steps = [("sums", k) for k in range(PRE)] + [("barrier",), ("g_own", 0, 0), ("g_far", 0), ("g_own", 0, 1)]
    steps += [("sums", k) for k in range(PRE, FILL)] + [("g_own", 1, 0)]
    steps += [("sums", k) for k in range(FILL, 16)]
    steps += [("g_relay", 0), ("g_z", 0, 0), ("send_roots",), ("g_z", 0, 1)] + [("g_far", 1)] * FAR_SOON
    steps += [("g_out", 0), ("g_zrelay", 0)] + [("g_far", 1)] * (not FAR_SOON) + [("g_relay", 1), ("g_own", 1, 1)]
    steps += [("inputs",), ("turn_roots",), ("scale", 0, 0), ("g_z", 1, 0), ("g_z", 1, 1), ("g_rest", 0), ("scale", 0, 1)]
    soon = 2 if REDUCE_Z[0] else 4
    steps += [("unit", 0, 0), ("g_out", 1), ("unit", 0, 1), *close(0, FAR[:soon]), ("g_zrelay", 1)]
    steps += [("unit", 0, 2), *close(0, FAR[soon:], NEAR[0]), ("unit", 0, 3), *close(0, NEAR[1]), ("scale", 1, 0)]
    steps += [*close(0, NEXT[0]) * (not STALL), ("g_rest", 1), ("scale", 1, 1), ("unit", 1, 0), *close(0, NEXT[0]) * STALL]
    steps += [("unit", 1, 1), *close(0, NEXT[1]), *close(1, FAR[:2]), ("unit", 1, 2), *close(1, NEAR[0])]
    steps += [("unit", 1, 3), *close(1, FAR[2:]), *close(0, HOME[0]), *close(1, NEXT[0], NEAR[1], NEXT[1], HOME[0])]
    steps += [*close(0, HOME[1])]
    steps += [("drain",), *close(1, HOME[1][:1]), ("output", 0), *close(1, HOME[1][1:]), ("output", 1), ("leave",)]
    return steps


def kernel(cnt_in, cols_in, feat, blocks, weight_in, bias_in, out, cnt, cols, weight, bias, o_v, blk, raw, pan, inv_t, rs_tx, rs_rx, inv_tx, inv_rx, part, sib_rx, acc,
           ab_rx, p_rx, m_rx, z_rx, agg, isem, osem, bsem, fsem, ssem, rsem):
    row, col, rep = lax.axis_index("row"), lax.axis_index("col"), lax.axis_index("rep")
    x, zh, zl, c = row // 2, row % 2, rep // 2, rep % 2
    q = col * 4 + rep
    n_chunk = 16
    brows = blk.shape[0] // n_chunk
    width = raw.shape[-1]

    def row_peer(i):
        return (lax.rem(row + i, 8), col, rep)

    def col_peer(i):
        p = lax.rem(q + i, 16)
        return (row, p // 4, p % 4)

    sib = (row, col, zl * 2 + 1 - c)
    y_next, y_prev = (row, lax.rem(col + 1, 4), rep), (row, lax.rem(col + 3, 4), rep)
    z_near = (row, col, (1 - zl) * 2 + c)
    x_next, x_prev = (lax.rem(x + 1, 4) * 2 + zh, col, rep), (lax.rem(x + 3, 4) * 2 + zh, col, rep)
    z_far = (x * 2 + 1 - zh, col, rep)

    def start(src, dst, sem):
        copy = pltpu.make_async_copy(src, dst, sem)
        copy.start()
        return copy

    feat_copies = [start(feat.at[:, pl.ds(h * width, width)], raw.at[h, row], fsem.at[h]) for h in range(HALVES)]
    cnt_copy = start(cnt_in, cnt, isem.at[0])

    block_copies = []

    def place_of(dy, dz, dc):
        return lax.rem(col + dy, 4), zl + dz - 2 * dz * zl, c + dc - 2 * dc * c

    def chunk_rows(k):
        y_, z_, c_ = place_of(*CHUNKS[k])
        return (y_ * 4 + z_ * 2 + c_) * brows

    def fetch(k):
        here = pl.ds(chunk_rows(k), brows)
        block_copies.append(start(blocks.at[here], blk.at[here], bsem.at[k % DEPTH]))

    barrier = pltpu.get_barrier_semaphore()
    fetch(0)
    for i in range(1, 8):
        pl.semaphore_signal(barrier, inc=1, device_id=row_peer(i), device_id_type=MESH)
    fetch(1)
    for i in range(1, 16):
        pl.semaphore_signal(barrier, inc=1, device_id=col_peer(i), device_id_type=MESH)
    for k in range(2, DEPTH):
        fetch(k)
    late_copies = [
        start(src, dst, isem.at[i + 1]) for i, (src, dst) in enumerate(((cols_in, cols), (weight_in, weight), (bias_in, bias)))
    ]

    numbers, pending = {}, [0, 0]

    def number(name):
        return numbers.setdefault(name, len(numbers))

    def send(name, src, dst, device, small=0):
        pltpu.make_async_remote_copy(
            src_ref=src, dst_ref=dst, send_sem=ssem.at[small], recv_sem=rsem.at[number(name)], device_id=device, device_id_type=MESH
        ).start()
        pending[small] += math.prod(src.shape) * src.dtype.itemsize

    def recv(name, place):
        pltpu.make_async_copy(place, place, rsem.at[number(name)]).wait()

    rs_tx[...] = jnp.zeros_like(rs_tx)
    for h in range(HALVES):
        pan[h, 32] = jnp.zeros((128, width), BF16)

    def row_sums(k):
        if k == 0:
            cnt_copy.wait()
        block_copies[k].wait()
        if k + DEPTH < n_chunk:
            fetch(k + DEPTH)
        first = chunk_rows(k)
        for j in range(brows):
            i = first + j
            live = cnt[0, i]
            total = jnp.zeros((128, 128), F32)
            for s in range(8):
                total = total + jnp.where(s < live, blk[i, s].astype(F32), 0.0)
            rs_tx[k, j : j + 1, :] = jnp.sum(total.T, axis=0, keepdims=True)
        if k >= PRE:
            send_sum(k)

    def send_sum(k):
        if k < n_chunk - 1:
            y_, z_, c_ = place_of(*CHUNKS[k])
            send("sums", rs_tx.at[k], rs_rx.at[q], (row, y_, z_ * 2 + c_), small=1)
        else:
            rs_rx[q] = rs_tx[k]

    half_z = GATHER_Z // 2
    mid = (pl.ds(256 - half_z, half_z), pl.ds(256, half_z))
    outer = (pl.ds(0, 256 - half_z), pl.ds(256 + half_z, 256 - half_z))
    side_rows = (pl.ds(0, 256), pl.ds(256, 256))
    at_next, at_prev, at_two = lax.rem(x + 1, 4), lax.rem(x + 3, 4), lax.rem(x + 2, 4)

    def piece(h, xs, z, rows):
        return raw.at[h, xs * 2 + z, rows]

    def copied(name, h, place, device):
        send((name, h), place, place, device)

    def outward(h, what, xs, side):
        if GATHER_Z < 512:
            copied(("out", what, side), h, piece(h, xs, zh, outer[side]), z_far)

    def gather_own(h, part):
        if part == 0:
            feat_copies[h].wait()
        copied(("own+", part), h, piece(h, x, zh, side_rows[part]), x_next)
        copied(("own-", 1 - part), h, piece(h, x, zh, side_rows[1 - part]), x_prev)

    def gather_far(h):
        for side in (0, 1):
            copied(("z", side), h, piece(h, x, zh, mid[side]), z_far)
        for side in (0, 1):
            outward(h, 0, x, side)

    def gather_relay(h):
        recv((("own+", 0), h), piece(h, at_prev, zh, side_rows[0]))
        copied("relay+", h, piece(h, at_prev, zh, side_rows[0]), x_next)
        recv((("own-", 1), h), piece(h, at_next, zh, side_rows[1]))
        copied("relay-", h, piece(h, at_next, zh, side_rows[1]), x_prev)
        outward(h, 1, at_prev, 0)
        outward(h, 2, at_next, 1)

    def gather_z(h, part):
        if part == 0:
            for side in (0, 1):
                recv((("z", side), h), piece(h, x, 1 - zh, mid[side]))
        copied(("z+", part), h, piece(h, x, 1 - zh, mid[part]), x_next)
        copied(("z-", 1 - part), h, piece(h, x, 1 - zh, mid[1 - part]), x_prev)

    def gather_out(h):
        recv((("own+", 1), h), piece(h, at_prev, zh, side_rows[1]))
        outward(h, 1, at_prev, 1)
        recv((("own-", 0), h), piece(h, at_next, zh, side_rows[0]))
        outward(h, 2, at_next, 0)

    def gather_zrelay(h):
        place = piece(h, at_prev, 1 - zh, mid[0])
        recv((("z+", 0), h), place)
        copied("zrelay+", h, place, x_next)
        place = piece(h, at_next, 1 - zh, mid[1])
        recv((("z-", 1), h), place)
        copied("zrelay-", h, place, x_prev)
        recv(("relay+", h), piece(h, at_two, zh, side_rows[0]))
        outward(h, 3, at_two, 0)
        recv(("relay-", h), piece(h, at_two, zh, side_rows[1]))
        outward(h, 3, at_two, 1)

    def gather_rest(h):
        recv((("z+", 1), h), piece(h, at_prev, 1 - zh, mid[1]))
        recv((("z-", 0), h), piece(h, at_next, 1 - zh, mid[0]))
        recv(("zrelay+", h), piece(h, at_two, 1 - zh, mid[0]))
        recv(("zrelay-", h), piece(h, at_two, 1 - zh, mid[1]))
        if GATHER_Z < 512:
            for what, xs in enumerate((x, at_prev, at_next, at_two)):
                for side in (0, 1):
                    recv((("out", what, side), h), piece(h, xs, 1 - zh, outer[side]))

    def scale(h, part):
        def group(xs, z):
            r = xs * 2 + z
            for j in range(4):
                rows = pl.ds(j * 128, 128)
                factor = inv_t[r, :, j : j + 1]
                pan[h, r * 4 + j] = (raw[h, r, rows, :].astype(F32) * factor).astype(BF16)

        if part == 0:
            for xs in (x, at_prev, at_next, at_two):
                group(xs, zh)
        else:
            for xs in (x, at_prev, at_next, at_two):
                group(xs, 1 - zh)

    def product(halves, slot, side, chip, core):
        first = (chip * 2 + core) * 4
        for j in range(4):
            i = first + j
            live = cnt[0, i]
            at = [jnp.where(s < live, cols[s, i], 32) for s in range(8)]
            picked = jnp.concatenate(
                [jnp.concatenate([pan[h, at[s]] for s in range(8)], axis=0) for h in halves], axis=1
            )
            tile = jnp.concatenate([blk[i, s] for s in range(8)], axis=1)
            total = jnp.dot(tile, picked, preferred_element_type=F32).astype(BF16)
            for n, h in enumerate(halves):
                part[h, side, slot, pl.ds(j * 128, 128), :] = total[:, n * width : (n + 1) * width]

    def unit(h, number):
        pairs = UNITS[number]
        for side, core in ((0, 1 - c), (1, c)):
            for n, (off, zc) in enumerate(pairs):
                chip = lax.rem(col + off, 4) * 2 + (zl if zc else 1 - zl)
                product((h,), number * 2 + n, side, chip, core)
        here = pl.ds(number * 2, 2)
        send(("sib", h, number), part.at[h, 0, here], sib_rx.at[h, here], sib)

    at_home = set()

    def moved(name, src, dst, device, lo, hi):
        if hi > lo:
            rows = pl.ds(lo, hi - lo)
            send(name, src.at[rows], dst.at[rows], device)

    def arrived(name, dst, lo, hi):
        if hi > lo:
            recv(name, dst.at[pl.ds(lo, hi - lo)])

    def close(h, off, zc, side):
        number, n = next((u, p.index((off, zc))) for u, p in enumerate(UNITS) if (off, zc) in p)
        slot = number * 2 + n
        last = zc == 1 and off == 0
        if (h, number) not in at_home:
            at_home.add((h, number))
            recv(("sib", h, number), sib_rx.at[h, pl.ds(number * 2, 2)])
        ra, rb = 256 - REDUCE_Z[h] // 2, 256 + REDUCE_Z[h] // 2
        outer_r, mid_r = ((0, ra), (ra, 256)) if side == 0 else ((rb, 512), (256, rb))
        lo, hi = (side * 256, side * 256 + 256) if zc else outer_r
        takes_ab = (off, side) in ((1, 0), (3, 1))
        if takes_ab:
            arrived(("ab", h, zc, side), ab_rx.at[h, zc], lo, hi)
        if off == 0:
            arrived(("p", h, zc, side), p_rx.at[h, zc], lo, hi)
            arrived(("m", h, zc, side), m_rx.at[h, zc], lo, hi)
        if zc == 1:
            arrived(("zm", h, off, side), z_rx.at[h, off], *mid_r)
            if off == 0:
                arrived(("zo", h, off, side), z_rx.at[h, off], *outer_r)
        for is_mid, (a, b) in enumerate((outer_r, mid_r)):
            if b == a:
                continue
            rows = pl.ds(a, b - a)
            round_y = zc == 1 or not is_mid
            total = part[h, 1, slot, rows, :].astype(F32) + sib_rx[h, slot, rows, :].astype(F32)
            if takes_ab and round_y:
                total = total + ab_rx[h, zc, rows, :].astype(F32)
            if off == 0 and round_y:
                total = total + p_rx[h, zc, rows, :].astype(F32) + m_rx[h, zc, rows, :].astype(F32)
            if zc == 1 and (is_mid or off == 0):
                total = total + z_rx[h, off, rows, :].astype(F32)
            if last:
                finish(h, a, b, total)
            else:
                acc[h, slot, rows, :] = total.astype(BF16)
        src = acc.at[h, slot]
        if zc == 0:
            moved(("zm", h, off, side), src, z_rx.at[h, off], z_near, *mid_r)
            if off == 0:
                moved(("zo", h, off, side), src, z_rx.at[h, off], z_near, *outer_r)
        if off == 2:
            moved(("ab", h, zc, side), src, ab_rx.at[h, zc], y_prev if side else y_next, lo, hi)
        if off == 1:
            moved(("p", h, zc, side), src, p_rx.at[h, zc], y_next, lo, hi)
        if off == 3:
            moved(("m", h, zc, side), src, m_rx.at[h, zc], y_prev, lo, hi)

    def finish(h, a, b, total):
        while a < b:
            j, end = a // 128, min(b, a // 128 * 128 + 128)
            factor = inv_t[8, a - j * 128 : end - j * 128, j : j + 1]
            own = pan[h, row * 4 + j, a - j * 128 : end - j * 128, :].astype(F32)
            agg[a:end, h * width : (h + 1) * width] = (factor * (total[: end - a] + own)).astype(BF16)
            total, a = total[end - a :], end

    def output(side):
        for j in (side * 2, side * 2 + 1):
            rows = pl.ds(j * 128, 128)
            mixed = jnp.dot(agg[rows, :], weight[...], preferred_element_type=F32) + bias[...]
            o_v[rows, :] = jnp.maximum(mixed, 0.0).astype(BF16)
            out_copies.append(start(o_v.at[rows], out.at[rows], osem.at[j]))

    out_copies = []

    def leave():
        for copy in out_copies:
            copy.wait()

    def drain():
        for n, (ref, unit_bytes) in enumerate(((blk, blk.shape[1] * 128 * 256), (o_v, o_v.shape[1] * 2))):
            assert pending[n] % unit_bytes == 0
            here = ref.at[pl.ds(0, pending[n] // unit_bytes)]
            pltpu.make_async_copy(here, here, ssem.at[n]).wait()

    def inputs():
        for copy in late_copies:
            copy.wait()

    def send_roots():
        recv("sums", rs_rx.at[pl.ds(0, 15)])
        degree = rs_rx[0]
        for i in range(1, 16):
            degree = degree + rs_rx[i]
        inv_tx[...] = lax.rsqrt(1.0 + degree)
        for i in range(1, 8):
            send("roots", inv_tx, inv_rx.at[row], row_peer(i), small=1)
        inv_rx[row] = inv_tx[...]

    def turn_roots():
        recv("roots", inv_rx.at[pl.ds(0, 7)])
        for r in range(8):
            inv_t[r] = inv_rx[r].T
        inv_t[8] = inv_tx[...].T

    def pass_barrier():
        pl.semaphore_wait(barrier, 22)
        for k in range(PRE):
            send_sum(k)

    work = {
        "sums": row_sums, "barrier": pass_barrier, "g_own": gather_own, "g_relay": gather_relay, "g_far": gather_far, "g_z": gather_z, "g_out": gather_out,
        "g_zrelay": gather_zrelay, "g_rest": gather_rest, "send_roots": send_roots,
        "turn_roots": turn_roots, "scale": scale, "unit": unit, "close": close, "output": output, "leave": leave,
        "drain": drain, "inputs": inputs,
    }
    for name, *args in schedule():
        with jax.named_scope("_".join(map(str, (name, *args)))) if SCOPES else contextlib.nullcontext():
            work[name](*args)
    assert len(numbers) == N_SEM, len(numbers)


def shards(features, blocks, block_cols, counts, weight, bias):
    rows, width = features.shape
    half = width // HALVES
    anywhere = pl.BlockSpec(memory_space=pl.ANY)
    dma = pltpu.SemaphoreType.DMA
    return pl.pallas_call(
        kernel,
        out_shape=jax.ShapeDtypeStruct((rows, width), BF16),
        in_specs=[anywhere] * 6,
        out_specs=anywhere,
        scratch_shapes=[
            pltpu.SMEM((1, blocks.shape[0]), jnp.int32),
            pltpu.SMEM((8, blocks.shape[0]), jnp.int32),
            pltpu.VMEM((width, width), BF16),
            pltpu.VMEM((1, width), F32),
            pltpu.VMEM((rows, width), BF16),
            pltpu.VMEM(blocks.shape, BF16),
            pltpu.VMEM((HALVES, 8, rows, half), BF16),
            pltpu.VMEM((HALVES, 33, 128, half), BF16),
            pltpu.VMEM((9, 128, 8), F32),
            pltpu.VMEM((16, 8, 128), F32),
            pltpu.VMEM((16, 8, 128), F32),
            pltpu.VMEM((8, 128), F32),
            pltpu.VMEM((8, 8, 128), F32),
            pltpu.VMEM((HALVES, 2, 8, rows, half), BF16),
            pltpu.VMEM((HALVES, 8, rows, half), BF16),
            pltpu.VMEM((HALVES, 8, rows, half), BF16),
            pltpu.VMEM((HALVES, 2, rows, half), BF16),
            pltpu.VMEM((HALVES, 2, rows, half), BF16),
            pltpu.VMEM((HALVES, 2, rows, half), BF16),
            pltpu.VMEM((HALVES, 4, rows, half), BF16),
            pltpu.VMEM((rows, width), BF16),
            dma((4,)), dma((4,)), dma((DEPTH,)), dma((HALVES,)), dma((2,)), dma((N_SEM,)),
        ],
        compiler_params=pltpu.CompilerParams(collective_id=0, has_side_effects=True, vmem_limit_bytes=58 << 20),
        cost_estimate=pl.CostEstimate(flops=4_300_000_000, bytes_accessed=17_000_000, transcendentals=1024),
    )(counts.T, block_cols.T, features, blocks, weight, bias.reshape(1, width))


def solution(mesh):
    return jax.shard_map(
        shards,
        mesh=mesh,
        in_specs=(
            P(("row", "col", "rep"), None),
            P("row", ("col", "rep"), None, None),
            P("row", ("col", "rep")),
            P("row", ("col", "rep")),
            P(),
            P(),
        ),
        out_specs=P(("row", "col", "rep"), None),
        check_vma=False,
    )
```

```python
import contextlib
import math

import jax
import jax.numpy as jnp
from jax import lax
from jax.experimental import pallas as pl
from jax.experimental.pallas import tpu as pltpu
from jax.sharding import PartitionSpec as P

MESH = pl.DeviceIdType.MESH
BF16, F32 = jnp.bfloat16, jnp.float32
HALVES = 2
SCOPES = False
PRE = 3
GATHER_Z = 384
STALL = 0
FAR_SOON = 1
REDUCE_Z = (0, 192)
DEPTH = 6
FILL = 9
CHUNKS = tuple((dy, dz, dc) for dz in (1, 0) for dy in (2, 1, 3, 0) for dc in (0, 1))
CHUNKS = CHUNKS[:-2] + CHUNKS[:-3:-1]
N_SEM = 66 + 16 * (GATHER_Z < 512) + 8 * sum(z > 0 for z in REDUCE_Z)
UNITS = (((2, 0), (2, 1)), ((1, 0), (3, 0)), ((1, 1), (3, 1)), ((0, 0), (0, 1)))
FAR = ((2, 0, 0), (2, 0, 1), (2, 1, 0), (2, 1, 1))
NEAR = [((1, zc, 1), (3, zc, 0)) for zc in (0, 1)]
NEXT = [((1, zc, 0), (3, zc, 1)) for zc in (0, 1)]
HOME = [((0, zc, 0), (0, zc, 1)) for zc in (0, 1)]


def schedule():
    def close(h, *groups):
        return [("close", h, *which) for group in groups for which in group]

    steps = [("sums", k) for k in range(PRE)] + [("barrier",), ("g_own", 0, 0), ("g_far", 0), ("g_own", 0, 1)]
    steps += [("sums", k) for k in range(PRE, FILL)] + [("g_own", 1, 0)]
    steps += [("sums", k) for k in range(FILL, 16)]
    steps += [("g_relay", 0), ("g_z", 0, 0), ("send_roots",), ("g_z", 0, 1)] + [("g_far", 1)] * FAR_SOON
    steps += [("g_out", 0), ("g_zrelay", 0)] + [("g_far", 1)] * (not FAR_SOON) + [("g_relay", 1), ("g_own", 1, 1)]
    steps += [("inputs",), ("turn_roots",), ("scale", 0, 0), ("g_z", 1, 0), ("g_z", 1, 1), ("g_rest", 0), ("scale", 0, 1)]
    soon = 2 if REDUCE_Z[0] else 4
    steps += [("unit", 0, 0), ("g_out", 1), ("unit", 0, 1), *close(0, FAR[:soon]), ("g_zrelay", 1)]
    steps += [("unit", 0, 2), *close(0, FAR[soon:], NEAR[0]), ("unit", 0, 3), *close(0, NEAR[1]), ("scale", 1, 0)]
    steps += [*close(0, NEXT[0]) * (not STALL), ("g_rest", 1), ("scale", 1, 1), ("unit", 1, 0), *close(0, NEXT[0]) * STALL]
    steps += [("unit", 1, 1), *close(0, NEXT[1]), *close(1, FAR[:2]), ("unit", 1, 2), *close(1, NEAR[0])]
    steps += [("unit", 1, 3), *close(1, FAR[2:]), *close(0, HOME[0]), *close(1, NEXT[0], NEAR[1], NEXT[1], HOME[0])]
    steps += [*close(0, HOME[1])]
    steps += [("drain",), *close(1, HOME[1][:1]), ("output", 0), *close(1, HOME[1][1:]), ("output", 1), ("leave",)]
    return steps


def kernel(cnt_in, cols_in, feat, blocks, weight_in, bias_in, out, cnt, cols, weight, bias, o_v, blk, raw, pan, inv_t, rs_tx, rs_rx, inv_tx, inv_rx, part, sib_rx, acc,
           ab_rx, p_rx, m_rx, z_rx, agg, isem, osem, bsem, fsem, ssem, rsem):
    row, col, rep = lax.axis_index("row"), lax.axis_index("col"), lax.axis_index("rep")
    x, zh, zl, c = row // 2, row % 2, rep // 2, rep % 2
    q = col * 4 + rep
    n_chunk = 16
    brows = blk.shape[0] // n_chunk
    width = raw.shape[-1]

    def row_peer(i):
        return (lax.rem(row + i, 8), col, rep)

    def col_peer(i):
        p = lax.rem(q + i, 16)
        return (row, p // 4, p % 4)

    sib = (row, col, zl * 2 + 1 - c)
    y_next, y_prev = (row, lax.rem(col + 1, 4), rep), (row, lax.rem(col + 3, 4), rep)
    z_near = (row, col, (1 - zl) * 2 + c)
    x_next, x_prev = (lax.rem(x + 1, 4) * 2 + zh, col, rep), (lax.rem(x + 3, 4) * 2 + zh, col, rep)
    z_far = (x * 2 + 1 - zh, col, rep)

    def start(src, dst, sem):
        copy = pltpu.make_async_copy(src, dst, sem)
        copy.start()
        return copy

    feat_copies = [start(feat.at[:, pl.ds(h * width, width)], raw.at[h, row], fsem.at[h]) for h in range(HALVES)]
    cnt_copy = start(cnt_in, cnt, isem.at[0])

    block_copies = []

    def place_of(dy, dz, dc):
        return lax.rem(col + dy, 4), zl + dz - 2 * dz * zl, c + dc - 2 * dc * c

    def chunk_rows(k):
        y_, z_, c_ = place_of(*CHUNKS[k])
        return (y_ * 4 + z_ * 2 + c_) * brows

    def fetch(k):
        here = pl.ds(chunk_rows(k), brows)
        block_copies.append(start(blocks.at[here], blk.at[here], bsem.at[k % DEPTH]))

    barrier = pltpu.get_barrier_semaphore()
    fetch(0)
    for i in range(1, 8):
        pl.semaphore_signal(barrier, inc=1, device_id=row_peer(i), device_id_type=MESH)
    fetch(1)
    for i in range(1, 16):
        pl.semaphore_signal(barrier, inc=1, device_id=col_peer(i), device_id_type=MESH)
    for k in range(2, DEPTH):
        fetch(k)
    late_copies = [
        start(src, dst, isem.at[i + 1]) for i, (src, dst) in enumerate(((cols_in, cols), (weight_in, weight), (bias_in, bias)))
    ]

    numbers, pending = {}, [0, 0]

    def number(name):
        return numbers.setdefault(name, len(numbers))

    def send(name, src, dst, device, small=0):
        pltpu.make_async_remote_copy(
            src_ref=src, dst_ref=dst, send_sem=ssem.at[small], recv_sem=rsem.at[number(name)], device_id=device, device_id_type=MESH
        ).start()
        pending[small] += math.prod(src.shape) * src.dtype.itemsize

    def recv(name, place):
        pltpu.make_async_copy(place, place, rsem.at[number(name)]).wait()

    rs_tx[...] = jnp.zeros_like(rs_tx)
    for h in range(HALVES):
        pan[h, 32] = jnp.zeros((128, width), BF16)

    def row_sums(k):
        if k == 0:
            cnt_copy.wait()
        block_copies[k].wait()
        if k + DEPTH < n_chunk:
            fetch(k + DEPTH)
        first = chunk_rows(k)
        for j in range(brows):
            i = first + j
            live = cnt[0, i]
            total = jnp.zeros((128, 128), F32)
            for s in range(8):
                total = total + jnp.where(s < live, blk[i, s].astype(F32), 0.0)
            rs_tx[k, j : j + 1, :] = jnp.sum(total.T, axis=0, keepdims=True)
        if k >= PRE:
            send_sum(k)

    def send_sum(k):
        if k < n_chunk - 1:
            y_, z_, c_ = place_of(*CHUNKS[k])
            send("sums", rs_tx.at[k], rs_rx.at[q], (row, y_, z_ * 2 + c_), small=1)
        else:
            rs_rx[q] = rs_tx[k]

    half_z = GATHER_Z // 2
    mid = (pl.ds(256 - half_z, half_z), pl.ds(256, half_z))
    outer = (pl.ds(0, 256 - half_z), pl.ds(256 + half_z, 256 - half_z))
    side_rows = (pl.ds(0, 256), pl.ds(256, 256))
    at_next, at_prev, at_two = lax.rem(x + 1, 4), lax.rem(x + 3, 4), lax.rem(x + 2, 4)

    def piece(h, xs, z, rows):
        return raw.at[h, xs * 2 + z, rows]

    def copied(name, h, place, device):
        send((name, h), place, place, device)

    def outward(h, what, xs, side):
        if GATHER_Z < 512:
            copied(("out", what, side), h, piece(h, xs, zh, outer[side]), z_far)

    def gather_own(h, part):
        if part == 0:
            feat_copies[h].wait()
        copied(("own+", part), h, piece(h, x, zh, side_rows[part]), x_next)
        copied(("own-", 1 - part), h, piece(h, x, zh, side_rows[1 - part]), x_prev)

    def gather_far(h):
        for side in (0, 1):
            copied(("z", side), h, piece(h, x, zh, mid[side]), z_far)
        for side in (0, 1):
            outward(h, 0, x, side)

    def gather_relay(h):
        recv((("own+", 0), h), piece(h, at_prev, zh, side_rows[0]))
        copied("relay+", h, piece(h, at_prev, zh, side_rows[0]), x_next)
        recv((("own-", 1), h), piece(h, at_next, zh, side_rows[1]))
        copied("relay-", h, piece(h, at_next, zh, side_rows[1]), x_prev)
        outward(h, 1, at_prev, 0)
        outward(h, 2, at_next, 1)

    def gather_z(h, part):
        if part == 0:
            for side in (0, 1):
                recv((("z", side), h), piece(h, x, 1 - zh, mid[side]))
        copied(("z+", part), h, piece(h, x, 1 - zh, mid[part]), x_next)
        copied(("z-", 1 - part), h, piece(h, x, 1 - zh, mid[1 - part]), x_prev)

    def gather_out(h):
        recv((("own+", 1), h), piece(h, at_prev, zh, side_rows[1]))
        outward(h, 1, at_prev, 1)
        recv((("own-", 0), h), piece(h, at_next, zh, side_rows[0]))
        outward(h, 2, at_next, 0)

    def gather_zrelay(h):
        place = piece(h, at_prev, 1 - zh, mid[0])
        recv((("z+", 0), h), place)
        copied("zrelay+", h, place, x_next)
        place = piece(h, at_next, 1 - zh, mid[1])
        recv((("z-", 1), h), place)
        copied("zrelay-", h, place, x_prev)
        recv(("relay+", h), piece(h, at_two, zh, side_rows[0]))
        outward(h, 3, at_two, 0)
        recv(("relay-", h), piece(h, at_two, zh, side_rows[1]))
        outward(h, 3, at_two, 1)

    def gather_rest(h):
        recv((("z+", 1), h), piece(h, at_prev, 1 - zh, mid[1]))
        recv((("z-", 0), h), piece(h, at_next, 1 - zh, mid[0]))
        recv(("zrelay+", h), piece(h, at_two, 1 - zh, mid[0]))
        recv(("zrelay-", h), piece(h, at_two, 1 - zh, mid[1]))
        if GATHER_Z < 512:
            for what, xs in enumerate((x, at_prev, at_next, at_two)):
                for side in (0, 1):
                    recv((("out", what, side), h), piece(h, xs, 1 - zh, outer[side]))

    def scale(h, part):
        def group(xs, z):
            r = xs * 2 + z
            for j in range(4):
                rows = pl.ds(j * 128, 128)
                factor = inv_t[r, :, j : j + 1]
                pan[h, r * 4 + j] = (raw[h, r, rows, :].astype(F32) * factor).astype(BF16)

        if part == 0:
            for xs in (x, at_prev, at_next, at_two):
                group(xs, zh)
        else:
            for xs in (x, at_prev, at_next, at_two):
                group(xs, 1 - zh)

    def product(halves, slot, side, chip, core):
        first = (chip * 2 + core) * 4
        for j in range(4):
            i = first + j
            live = cnt[0, i]
            at = [jnp.where(s < live, cols[s, i], 32) for s in range(8)]
            picked = jnp.concatenate(
                [jnp.concatenate([pan[h, at[s]] for s in range(8)], axis=0) for h in halves], axis=1
            )
            tile = jnp.concatenate([blk[i, s] for s in range(8)], axis=1)
            total = jnp.dot(tile, picked, preferred_element_type=F32).astype(BF16)
            for n, h in enumerate(halves):
                part[h, side, slot, pl.ds(j * 128, 128), :] = total[:, n * width : (n + 1) * width]

    def unit(h, number):
        pairs = UNITS[number]
        for side, core in ((0, 1 - c), (1, c)):
            for n, (off, zc) in enumerate(pairs):
                chip = lax.rem(col + off, 4) * 2 + (zl if zc else 1 - zl)
                product((h,), number * 2 + n, side, chip, core)
        here = pl.ds(number * 2, 2)
        send(("sib", h, number), part.at[h, 0, here], sib_rx.at[h, here], sib)

    at_home = set()

    def moved(name, src, dst, device, lo, hi):
        if hi > lo:
            rows = pl.ds(lo, hi - lo)
            send(name, src.at[rows], dst.at[rows], device)

    def arrived(name, dst, lo, hi):
        if hi > lo:
            recv(name, dst.at[pl.ds(lo, hi - lo)])

    def close(h, off, zc, side):
        number, n = next((u, p.index((off, zc))) for u, p in enumerate(UNITS) if (off, zc) in p)
        slot = number * 2 + n
        last = zc == 1 and off == 0
        if (h, number) not in at_home:
            at_home.add((h, number))
            recv(("sib", h, number), sib_rx.at[h, pl.ds(number * 2, 2)])
        ra, rb = 256 - REDUCE_Z[h] // 2, 256 + REDUCE_Z[h] // 2
        outer_r, mid_r = ((0, ra), (ra, 256)) if side == 0 else ((rb, 512), (256, rb))
        lo, hi = (side * 256, side * 256 + 256) if zc else outer_r
        takes_ab = (off, side) in ((1, 0), (3, 1))
        if takes_ab:
            arrived(("ab", h, zc, side), ab_rx.at[h, zc], lo, hi)
        if off == 0:
            arrived(("p", h, zc, side), p_rx.at[h, zc], lo, hi)
            arrived(("m", h, zc, side), m_rx.at[h, zc], lo, hi)
        if zc == 1:
            arrived(("zm", h, off, side), z_rx.at[h, off], *mid_r)
            if off == 0:
                arrived(("zo", h, off, side), z_rx.at[h, off], *outer_r)
        for is_mid, (a, b) in enumerate((outer_r, mid_r)):
            if b == a:
                continue
            rows = pl.ds(a, b - a)
            round_y = zc == 1 or not is_mid
            total = part[h, 1, slot, rows, :].astype(F32) + sib_rx[h, slot, rows, :].astype(F32)
            if takes_ab and round_y:
                total = total + ab_rx[h, zc, rows, :].astype(F32)
            if off == 0 and round_y:
                total = total + p_rx[h, zc, rows, :].astype(F32) + m_rx[h, zc, rows, :].astype(F32)
            if zc == 1 and (is_mid or off == 0):
                total = total + z_rx[h, off, rows, :].astype(F32)
            if last:
                finish(h, a, b, total)
            else:
                acc[h, slot, rows, :] = total.astype(BF16)
        src = acc.at[h, slot]
        if zc == 0:
            moved(("zm", h, off, side), src, z_rx.at[h, off], z_near, *mid_r)
            if off == 0:
                moved(("zo", h, off, side), src, z_rx.at[h, off], z_near, *outer_r)
        if off == 2:
            moved(("ab", h, zc, side), src, ab_rx.at[h, zc], y_prev if side else y_next, lo, hi)
        if off == 1:
            moved(("p", h, zc, side), src, p_rx.at[h, zc], y_next, lo, hi)
        if off == 3:
            moved(("m", h, zc, side), src, m_rx.at[h, zc], y_prev, lo, hi)

    def finish(h, a, b, total):
        while a < b:
            j, end = a // 128, min(b, a // 128 * 128 + 128)
            factor = inv_t[8, a - j * 128 : end - j * 128, j : j + 1]
            own = pan[h, row * 4 + j, a - j * 128 : end - j * 128, :].astype(F32)
            agg[a:end, h * width : (h + 1) * width] = (factor * (total[: end - a] + own)).astype(BF16)
            total, a = total[end - a :], end

    def output(side):
        for j in (side * 2, side * 2 + 1):
            rows = pl.ds(j * 128, 128)
            mixed = jnp.dot(agg[rows, :], weight[...], preferred_element_type=F32) + bias[...]
            o_v[rows, :] = jnp.maximum(mixed, 0.0).astype(BF16)
            out_copies.append(start(o_v.at[rows], out.at[rows], osem.at[j]))

    out_copies = []

    def leave():
        for copy in out_copies:
            copy.wait()

    def drain():
        for n, (ref, unit_bytes) in enumerate(((blk, blk.shape[1] * 128 * 256), (o_v, o_v.shape[1] * 2))):
            assert pending[n] % unit_bytes == 0
            here = ref.at[pl.ds(0, pending[n] // unit_bytes)]
            pltpu.make_async_copy(here, here, ssem.at[n]).wait()

    def inputs():
        for copy in late_copies:
            copy.wait()

    def send_roots():
        recv("sums", rs_rx.at[pl.ds(0, 15)])
        degree = rs_rx[0]
        for i in range(1, 16):
            degree = degree + rs_rx[i]
        inv_tx[...] = lax.rsqrt(1.0 + degree)
        for i in range(1, 8):
            send("roots", inv_tx, inv_rx.at[row], row_peer(i), small=1)
        inv_rx[row] = inv_tx[...]

    def turn_roots():
        recv("roots", inv_rx.at[pl.ds(0, 7)])
        for r in range(8):
            inv_t[r] = inv_rx[r].T
        inv_t[8] = inv_tx[...].T

    def pass_barrier():
        pl.semaphore_wait(barrier, 22)
        for k in range(PRE):
            send_sum(k)

    work = {
        "sums": row_sums, "barrier": pass_barrier, "g_own": gather_own, "g_relay": gather_relay, "g_far": gather_far, "g_z": gather_z, "g_out": gather_out,
        "g_zrelay": gather_zrelay, "g_rest": gather_rest, "send_roots": send_roots,
        "turn_roots": turn_roots, "scale": scale, "unit": unit, "close": close, "output": output, "leave": leave,
        "drain": drain, "inputs": inputs,
    }
    for name, *args in schedule():
        with jax.named_scope("_".join(map(str, (name, *args)))) if SCOPES else contextlib.nullcontext():
            work[name](*args)
    assert len(numbers) == N_SEM, len(numbers)


def shards(features, blocks, block_cols, counts, weight, bias):
    rows, width = features.shape
    half = width // HALVES
    anywhere = pl.BlockSpec(memory_space=pl.ANY)
    dma = pltpu.SemaphoreType.DMA
    return pl.pallas_call(
        kernel,
        out_shape=jax.ShapeDtypeStruct((rows, width), BF16),
        in_specs=[anywhere] * 6,
        out_specs=anywhere,
        scratch_shapes=[
            pltpu.SMEM((1, blocks.shape[0]), jnp.int32),
            pltpu.SMEM((8, blocks.shape[0]), jnp.int32),
            pltpu.VMEM((width, width), BF16),
            pltpu.VMEM((1, width), F32),
            pltpu.VMEM((rows, width), BF16),
            pltpu.VMEM(blocks.shape, BF16),
            pltpu.VMEM((HALVES, 8, rows, half), BF16),
            pltpu.VMEM((HALVES, 33, 128, half), BF16),
            pltpu.VMEM((9, 128, 8), F32),
            pltpu.VMEM((16, 8, 128), F32),
            pltpu.VMEM((16, 8, 128), F32),
            pltpu.VMEM((8, 128), F32),
            pltpu.VMEM((8, 8, 128), F32),
            pltpu.VMEM((HALVES, 2, 8, rows, half), BF16),
            pltpu.VMEM((HALVES, 8, rows, half), BF16),
            pltpu.VMEM((HALVES, 8, rows, half), BF16),
            pltpu.VMEM((HALVES, 2, rows, half), BF16),
            pltpu.VMEM((HALVES, 2, rows, half), BF16),
            pltpu.VMEM((HALVES, 2, rows, half), BF16),
            pltpu.VMEM((HALVES, 4, rows, half), BF16),
            pltpu.VMEM((rows, width), BF16),
            dma((4,)), dma((4,)), dma((DEPTH,)), dma((HALVES,)), dma((2,)), dma((N_SEM,)),
        ],
        compiler_params=pltpu.CompilerParams(collective_id=0, has_side_effects=True, vmem_limit_bytes=58 << 20),
        cost_estimate=pl.CostEstimate(flops=4_300_000_000, bytes_accessed=17_000_000, transcendentals=1024),
    )(counts.T, block_cols.T, features, blocks, weight, bias.reshape(1, width))


def solution(mesh):
    return jax.shard_map(
        shards,
        mesh=mesh,
        in_specs=(
            P(("row", "col", "rep"), None),
            P("row", ("col", "rep"), None, None),
            P("row", ("col", "rep")),
            P("row", ("col", "rep")),
            P(),
            P(),
        ),
        out_specs=P(("row", "col", "rep"), None),
        check_vma=False,
    )
```
